32 devices in a mesh: groups: 2 (over y), expert: 8 (over z, x), head: 2 (over core).
Axes of the slice: x: 2, y: 2, z: 4, core: 2. Of those that a mesh axis runs over, the one named last changes fastest.
Arguments:
- stream: bfloat16 [2, 16, 4096], P(None, ('groups', 'expert')), parts along dimension 1, may hold values from -6 to 6
- heads_in: bfloat16 [2, 16, 8192], P(None, ('groups', 'expert'), 'head'), parts along dimension 1, may hold values from -6 to 6
- heads_gate: bfloat16 [2, 16, 8192], P(None, ('groups', 'expert'), 'head'), parts along dimension 1, may hold values from -6 to 6
- write_key: bfloat16 [2, 16, 64], P(None, ('groups', 'expert')), parts along dimension 1, may hold values from -6 to 6
- read_query: bfloat16 [2, 16, 64], P(None, ('groups', 'expert')), parts along dimension 1, may hold values from -0.75 to 0.75
- step_size: float32 [2, 16, 128], P(None, ('groups', 'expert'), 'head'), parts along dimension 1, may hold values from 0.05 to 1
- state_cache: bfloat16 [16, 128, 4096], P(('groups', 'expert'), 'head'), parts along dimension 0, may hold values from -6 to 6
- decay_rate: float32 [128], P('head'), may hold values from 0.5 to 8
- skip_gain: float32 [128], P('head'), may hold values from 0.5 to 1.5
- out_weight: bfloat16 [8192, 4096], P('head', 'expert'), may hold values from -0.0625 to 0.0625
- norm_gain: float32 [4096], replicated, may hold values from 0.5 to 1.5
- up_weight: bfloat16 [4096, 65536], P(None, ('expert', 'head')), may hold values from -0.09375 to 0.09375
- down_weight: bfloat16 [65536, 4096], P(('expert', 'head')), may hold values from -0.046875 to 0.046875
- expert_ids: int32 [2, 16, 2], P(None, ('groups', 'expert')), parts along dimension 1, may hold values from 0 to 3, all different within a row
- expert_gates: bfloat16 [2, 16, 2], P(None, ('groups', 'expert')), parts along dimension 1, may hold values from 0.19921875 to 1
Outputs:
- layer_out: bfloat16 [2, 16, 4096], P(None, ('groups', 'expert')), parts along dimension 1
The draws below stay inside these ranges and needn't reach their ends.
There are 2 independent parts, one for each index of `groups`. The reference program is written for one: setup_inputs(seed, part) draws one part's arguments, and reference() takes and returns one part's arrays. A program takes and returns all parts, laid end to end along the dimension named above; an argument that names none is the same for every part. Nothing has to cross between parts.
Inputs may be any that keep to these rules, and one draw needn't show every extreme that they name: `expert_ids`: each token names 2 different experts.
All inputs are finite; a program needn't handle non-finite values.
Results may differ from the reference program's by a relative error of at most 0.0056.
Values may be sent and summed in bfloat16 or wider, within the bound.
A program may use at most 192 MiB of HBM per device.

```python
import math
import jax
import jax.numpy as jnp
from jax import lax

D = 4096
H = 128
P_SIZE = 64
N = 64
EXPERTS = 4
TOP = 2
FF = 16384
STEPS = 2
TOKENS = 8


def level_of(own_key, shape, split, least, largest):
    level = 1.0
    for axis_at, shards_of in split:
        heights = jax.random.uniform(jax.random.fold_in(jax.random.fold_in(own_key, 6), axis_at), (shards_of,), jnp.float32, least / len(split), largest / len(split))
        level = level * jnp.repeat(jnp.exp(heights), shape[axis_at] // shards_of).reshape((-1,) + (1,) * (len(shape) - 1 - axis_at))
    return level


def choose_distinct(rng, rows, count, top, lift):
    ranking = jax.random.permutation(jax.random.fold_in(rng, 1), count)
    boost = ranking
    for power in range(3):
        boost = boost * boost // count
    boost = boost * lift // count
    tickets = jax.random.randint(jax.random.fold_in(rng, 2), (rows, count), 0, 4096) + boost
    fixed_rows = jax.random.permutation(jax.random.fold_in(rng, 3), rows)[jnp.arange(count) % rows]
    tickets = jnp.where(jnp.arange(rows)[:, None] == fixed_rows[None, :], 1 << 14, tickets)
    score = tickets * count + jnp.arange(count)
    return lax.top_k(score.astype(jnp.int32), top)[1].astype(jnp.int32)


def centred(rng, extent, scale, reach, cuts=(), dtype=jnp.bfloat16):
    result = jax.random.normal(rng, extent, jnp.float32) * scale
    if len(cuts) > 0:
        result = level_of(rng, extent, cuts, -0.22, 0.18) * result
    return jnp.clip(result, min=-reach, max=reach).astype(dtype)


def setup_inputs(seed: int = 0, part: int = 0) -> dict:
    key_of = jax.random.split(jax.random.key(seed), 16)
    part_keys = jax.random.split(jax.random.fold_in(key_of[15], part), 16)
    return {
        "stream": centred(part_keys[0], (STEPS, TOKENS, D), 1.0, 6.0, ((1, 8),)),
        "heads_in": centred(part_keys[1], (STEPS, TOKENS, H * P_SIZE), 1.0, 6.0, ((1, 8), (2, 2))),
        "heads_gate": centred(part_keys[2], (STEPS, TOKENS, H * P_SIZE), 1.0, 6.0, ((1, 8), (2, 2))),
        "write_key": centred(part_keys[3], (STEPS, TOKENS, N), 1.0, 6.0, ((1, 8),)),
        "read_query": centred(part_keys[4], (STEPS, TOKENS, N), N ** -0.5, 0.75, ((1, 8),)),
        "step_size": jnp.clip(jnp.exp(math.log(1.0) - 2.9957323 * jax.random.uniform(part_keys[5], (STEPS, TOKENS, H), jnp.float32) ** level_of(part_keys[5], (STEPS, TOKENS, H), ((1, 8), (2, 2)), -0.2, 0.2)), 0.05, 1.0),
        "state_cache": centred(part_keys[6], (TOKENS, H, P_SIZE * N), 1.0, 6.0, ((0, 8), (1, 2))),
        "decay_rate": jnp.clip(jnp.exp(math.log(8.0) - 2.7725887 * jax.random.uniform(key_of[7], (H,), jnp.float32) ** level_of(key_of[7], (H,), ((0, 2),), -0.2, 0.2)), 0.5, 8.0),
        "skip_gain": jnp.clip(0.5 + 1.0 * jax.random.uniform(key_of[8], (H,), jnp.float32) ** level_of(key_of[8], (H,), ((0, 2),), -0.2, 0.2), 0.5, 1.5),
        "out_weight": centred(key_of[9], (H * P_SIZE, D), (H * P_SIZE) ** -0.5, 0.0625, ((0, 2), (1, 8))),
        "norm_gain": jnp.clip(jax.random.uniform(key_of[10], (D,), jnp.float32, 0.5, 1.5), 0.5, 1.5),
        "up_weight": centred(key_of[11], (D, EXPERTS * FF), D ** -0.5, 0.09375, ((1, 16),)),
        "down_weight": centred(key_of[12], (EXPERTS * FF, D), FF ** -0.5, 0.046875, ((0, 16),)),
        "expert_ids": choose_distinct(part_keys[13], STEPS * TOKENS, EXPERTS, TOP, 0).reshape((STEPS, TOKENS, TOP)),
        "expert_gates": jnp.clip(0.19921875 + 0.80078125 * jax.random.uniform(part_keys[14], (STEPS, TOKENS, TOP), jnp.float32) ** level_of(part_keys[14], (STEPS, TOKENS, TOP), ((1, 8),), -0.2, 0.2), 0.19921875, 1.0).astype(jnp.bfloat16),
    }


EPSILON = 1e-05

def reference(stream, heads_in, heads_gate, write_key, read_query, step_size, state_cache, decay_rate, skip_gain, out_weight, norm_gain, up_weight, down_weight, expert_ids, expert_gates):
    state = state_cache.astype(jnp.float32).reshape(TOKENS, H, P_SIZE, N)
    experts = lax.broadcasted_iota(jnp.int32, (1, 1, EXPERTS), 2)
    results = []
    for step in range(STEPS):
        values = heads_in[step].astype(jnp.float32).reshape(TOKENS, H, P_SIZE)
        delta = step_size[step]
        keys = write_key[step].astype(jnp.float32)
        query = read_query[step].astype(jnp.float32)
        factor = jnp.exp(-delta * decay_rate[None, :])
        state = factor[:, :, None, None] * state + (delta[:, :, None] * values)[:, :, :, None] * keys[:, None, None, :]
        read = jnp.einsum('thpn,tn->thp', state, query, precision=lax.Precision.HIGHEST) + skip_gain[None, :, None] * values
        gate = heads_gate[step].astype(jnp.float32).reshape(TOKENS, H, P_SIZE)
        mixer = (read * jax.nn.silu(gate)).reshape(TOKENS, H * P_SIZE).astype(jnp.bfloat16)
        mixed = jnp.dot(mixer, out_weight, preferred_element_type=jnp.float32)
        middle = (stream[step].astype(jnp.float32) + mixed).astype(jnp.bfloat16)
        wide = middle.astype(jnp.float32)
        scale = lax.rsqrt(lax.optimization_barrier(jnp.mean(wide * wide, axis=-1, keepdims=True)) + EPSILON)
        normed = (wide * scale * norm_gain[None, :]).astype(jnp.bfloat16)
        table = lax.optimization_barrier(jnp.sum(jnp.where(expert_ids[step][:, :, None] == experts, expert_gates[step][:, :, None].astype(jnp.float32), jnp.float32(0.0)), axis=1)).astype(jnp.bfloat16)
        lifted = jnp.dot(normed, up_weight, preferred_element_type=jnp.float32).reshape(TOKENS, EXPERTS, FF)
        hidden = (jax.nn.gelu(lifted) * table.astype(jnp.float32)[:, :, None]).reshape(TOKENS, EXPERTS * FF).astype(jnp.bfloat16)
        moe = jnp.dot(hidden, down_weight, preferred_element_type=jnp.float32)
        results.append((wide + moe).astype(jnp.bfloat16))
    return jnp.stack(results)
```

```python
import jax
import jax.numpy as jnp
from jax import lax
from jax.sharding import PartitionSpec as P

P_SIZE = 64
N = 64
EXPERTS = 4
FF = 16384
STEPS = 2


EPSILON = 1e-05


def finish(
    mixer, stream, expert_ids, expert_gates, out_weight, norm_gain, up_weight, down_weight, owner
):
    partial_out = jnp.einsum(
        "srk,kc->src",
        lax.all_gather(mixer, "expert", axis=1, tiled=True),
        out_weight,
        preferred_element_type=jnp.float32,
    )
    summed = lax.psum(partial_out, "head")
    mixed = lax.all_to_all(summed, "expert", split_axis=1, concat_axis=2, tiled=True)
    middle = (stream.astype(jnp.float32) + mixed).astype(jnp.bfloat16)
    wide = middle.astype(jnp.float32)
    scale = lax.rsqrt(jnp.mean(wide * wide, axis=-1, keepdims=True) + EPSILON)
    normed = (wide * scale * norm_gain[None, None, :]).astype(jnp.bfloat16)
    experts = lax.broadcasted_iota(jnp.int32, (1, 1, 1, EXPERTS), 3)
    table = jnp.sum(
        jnp.where(
            expert_ids[:, :, :, None] == experts,
            expert_gates[:, :, :, None].astype(jnp.float32),
            jnp.float32(0.0),
        ),
        axis=2,
    ).astype(jnp.bfloat16)
    every_token, every_table = (
        lax.all_gather(normed, "expert", axis=1, tiled=True),
        lax.all_gather(table, "expert", axis=1, tiled=True),
    )
    picker = lax.broadcasted_iota(jnp.int32, (1, 1, EXPERTS), 2) == owner
    weight_row = jnp.sum(
        jnp.where(picker, every_table.astype(jnp.float32), jnp.float32(0.0)), axis=2
    )
    lifted = jnp.einsum("std,dc->tsc", every_token, up_weight, preferred_element_type=jnp.float32)
    hidden = (jax.nn.gelu(lifted) * jnp.transpose(weight_row)[:, :, None]).astype(jnp.bfloat16)
    combined = lax.psum_scatter(
        jnp.einsum("tsc,cd->tsd", hidden, down_weight, preferred_element_type=jnp.float32),
        "expert",
        scatter_dimension=0,
        tiled=True,
    )
    total = lax.psum(combined, "head")
    return (wide + jnp.transpose(total, (1, 0, 2))).astype(jnp.bfloat16)


def on_device(
    stream,
    heads_in,
    heads_gate,
    write_key,
    read_query,
    step_size,
    state_cache,
    decay_rate,
    skip_gain,
    out_weight,
    norm_gain,
    up_weight,
    down_weight,
    expert_ids,
    expert_gates,
):
    local_rows = heads_in.shape[1]
    local_width = heads_in.shape[2]
    local_heads = decay_rate.shape[0]
    state = state_cache.astype(jnp.float32).reshape(local_rows, local_heads, P_SIZE, N)
    position = lax.axis_index("expert") * lax.axis_size("head") + lax.axis_index("head")
    owner = position * up_weight.shape[1] // FF
    mixers = []
    for step in range(STEPS):
        values = heads_in[step].astype(jnp.float32).reshape(local_rows, local_heads, P_SIZE)
        delta = step_size[step]
        keys = write_key[step].astype(jnp.float32)
        query = read_query[step].astype(jnp.float32)
        factor = jnp.exp(-delta * decay_rate[None, :])
        state = (
            factor[:, :, None, None] * state
            + (delta[:, :, None] * values)[:, :, :, None] * keys[:, None, None, :]
        )
        read = (
            jnp.einsum("thpn,tn->thp", state, query, precision=lax.Precision.HIGHEST)
            + skip_gain[None, :, None] * values
        )
        gate = heads_gate[step].astype(jnp.float32).reshape(local_rows, local_heads, P_SIZE)
        mixers.append((read * jax.nn.silu(gate)).reshape(local_rows, local_width).astype(jnp.bfloat16))
    return finish(
        jnp.stack(mixers),
        stream,
        expert_ids,
        expert_gates,
        out_weight,
        norm_gain,
        up_weight,
        down_weight,
        owner,
    )


def solution(mesh):
    placed = (
        P(None, ("groups", "expert"), None),
        P(None, ("groups", "expert"), "head"),
        P(None, ("groups", "expert"), "head"),
        P(None, ("groups", "expert"), None),
        P(None, ("groups", "expert"), None),
        P(None, ("groups", "expert"), "head"),
        P(("groups", "expert"), "head", None),
        P("head"),
        P("head"),
        P("head", "expert"),
        P(),
        P(None, ("expert", "head")),
        P(("expert", "head"), None),
        P(None, ("groups", "expert"), None),
        P(None, ("groups", "expert"), None),
    )
    return jax.shard_map(
        on_device,
        mesh=mesh,
        in_specs=placed,
        out_specs=P(None, ("groups", "expert"), None),
        check_vma=False,
    )
```

```python
import functools
import jax
import jax.numpy as jnp
from jax import lax
from jax.experimental import pallas as pl
from jax.experimental.pallas import tpu as pltpu
from jax.sharding import PartitionSpec as P

P_SIZE = 64
N = 64
EXPERTS = 4
FF = 16384
STEPS = 2


EPSILON = 1e-05


def finish(
    mixer, stream, expert_ids, expert_gates, out_weight, norm_gain, up_weight, down_weight, owner
):
    partial_out = jnp.einsum(
        "srk,kc->src",
        lax.all_gather(mixer, "expert", axis=1, tiled=True),
        out_weight,
        preferred_element_type=jnp.float32,
    )
    summed = lax.psum(partial_out, "head")
    mixed = lax.all_to_all(summed, "expert", split_axis=1, concat_axis=2, tiled=True)
    middle = (stream.astype(jnp.float32) + mixed).astype(jnp.bfloat16)
    wide = middle.astype(jnp.float32)
    scale = lax.rsqrt(jnp.mean(wide * wide, axis=-1, keepdims=True) + EPSILON)
    normed = (wide * scale * norm_gain[None, None, :]).astype(jnp.bfloat16)
    experts = lax.broadcasted_iota(jnp.int32, (1, 1, 1, EXPERTS), 3)
    table = jnp.sum(
        jnp.where(
            expert_ids[:, :, :, None] == experts,
            expert_gates[:, :, :, None].astype(jnp.float32),
            jnp.float32(0.0),
        ),
        axis=2,
    ).astype(jnp.bfloat16)
    every_token, every_table = (
        lax.all_gather(normed, "expert", axis=1, tiled=True),
        lax.all_gather(table, "expert", axis=1, tiled=True),
    )
    picker = lax.broadcasted_iota(jnp.int32, (1, 1, EXPERTS), 2) == owner
    weight_row = jnp.sum(
        jnp.where(picker, every_table.astype(jnp.float32), jnp.float32(0.0)), axis=2
    )
    lifted = jnp.einsum("std,dc->tsc", every_token, up_weight, preferred_element_type=jnp.float32)
    hidden = (jax.nn.gelu(lifted) * jnp.transpose(weight_row)[:, :, None]).astype(jnp.bfloat16)
    combined = lax.psum_scatter(
        jnp.einsum("tsc,cd->tsd", hidden, down_weight, preferred_element_type=jnp.float32),
        "expert",
        scatter_dimension=0,
        tiled=True,
    )
    total = lax.psum(combined, "head")
    return (wide + jnp.transpose(total, (1, 0, 2))).astype(jnp.bfloat16)


LANES = 128
WIDE = 512
RING = 13


def layer_kernel(
    n,
    mixer_ref, aux_ref, gain_ref, out_w, up_w, down_w,
    total_ref, middle_ref,
    ring, mixers, auxes, unpacked, rows, mine, theirs, blocks, normed, wide, hidden,
    stage, packed, parts, halves,
    weight_sem, mix_send, mix_recv, aux_send, aux_recv, core_send, core_recv,
    mid_send, mid_recv, part_send, part_recv, half_send, half_recv,
):
    me = lax.axis_index("expert")
    other = 1 - lax.axis_index("head")
    ups = up_w.shape[1] // WIDE
    downs = down_w.shape[1] // WIDE
    pairs = downs // 2
    columns = n * WIDE

    def block(i):
        return pl.ds(pl.multiple_of(i * WIDE, WIDE), WIDE)

    def out_copy():
        return pltpu.make_async_copy(out_w, ring.at[0], weight_sem.at[0])

    def up_copy(i):
        return pltpu.make_async_copy(up_w.at[:, block(i)], ring.at[1 + i], weight_sem.at[1 + i])

    def down_copy(i):
        at = 1 + ups + i
        return pltpu.make_async_copy(
            down_w.at[:, block(i)], ring.at[lax.rem(at, RING)], weight_sem.at[at]
        )

    early = RING - 1 - ups
    out_copy().start()
    pl.loop(0, ups)(lambda i: up_copy(i).start())
    pl.loop(0, early)(lambda i: down_copy(i).start())

    barrier = pltpu.get_barrier_semaphore()
    for d in range(1, n):
        pl.semaphore_signal(
            barrier, inc=1, device_id={"expert": lax.rem(me + d, n)},
            device_id_type=pl.DeviceIdType.MESH,
        )
    pl.semaphore_signal(
        barrier, inc=1, device_id={"head": other}, device_id_type=pl.DeviceIdType.MESH
    )
    pl.semaphore_wait(barrier, n)

    def to_peer(d, src, dst, send, recv):
        return pltpu.make_async_remote_copy(
            src_ref=src, dst_ref=dst, send_sem=send, recv_sem=recv,
            device_id={"expert": lax.rem(me + d, n)}, device_id_type=pl.DeviceIdType.MESH,
        )

    def to_core(src, dst, send, recv):
        return pltpu.make_async_remote_copy(
            src_ref=src, dst_ref=dst, send_sem=send, recv_sem=recv,
            device_id={"head": other}, device_id_type=pl.DeviceIdType.MESH,
        )

    mix = [
        to_peer(d, mixer_ref, mixers.at[me], mix_send.at[d], mix_recv.at[d]) for d in range(1, n)
    ]
    aux = [
        to_peer(d, aux_ref.at[lax.rem(me + d, n)], auxes.at[me], aux_send.at[d], aux_recv.at[d])
        for d in range(1, n)
    ]
    for copy in mix + aux:
        copy.start()
    mixers[me] = mixer_ref[...]
    auxes[me] = aux_ref[me]
    for copy in mix:
        copy.wait()
    unpacked[...] = mixers[...].astype(jnp.float32)
    for step in range(STEPS):
        for k in range(n):
            rows[step * n : (step + 1) * n, k * WIDE : (k + 1) * WIDE] = unpacked[:, step * n + k, :]

    out_copy().wait()
    mine[...] = jnp.dot(
        rows[...].astype(jnp.bfloat16), ring[0], preferred_element_type=jnp.float32
    )
    down_copy(early).start()
    swap = to_core(mine, theirs, core_send, core_recv)
    swap.start()
    for copy in aux:
        copy.wait()
    swap.wait()
    per = WIDE // LANES
    for step in range(STEPS):
        for q in range(per):
            at = slice(step * n, (step + 1) * n), slice(q * LANES, (q + 1) * LANES)
            mine[at] = auxes[:, step * per + q, :] + (mine[at] + theirs[at])
    blocks[me] = mine[...].astype(jnp.bfloat16)
    mid = [
        to_peer(d, blocks.at[me], blocks.at[me], mid_send.at[d], mid_recv.at[d])
        for d in range(1, n)
    ]
    for copy in mid:
        copy.start()
    for copy in mid:
        copy.wait()
    square = jnp.zeros((STEPS * n, WIDE), jnp.float32)
    for k in range(n):
        part = blocks[k].astype(jnp.float32)
        wide[:, k * WIDE : (k + 1) * WIDE] = part
        square += part * part
    scale = lax.rsqrt(jnp.sum(square, axis=-1, keepdims=True) / columns + EPSILON)
    for k in range(n):
        at = slice(None), slice(k * WIDE, (k + 1) * WIDE)
        normed[at] = (wide[at] * scale * gain_ref[:, k * WIDE : (k + 1) * WIDE]).astype(jnp.bfloat16)
    for step in range(STEPS):
        middle_ref[step : step + 1, :] = wide[pl.ds(step * n + me, 1), :]
    first = STEPS * per
    weight = jnp.concatenate(
        [auxes[:, first + step, :] for step in range(STEPS)], axis=0
    )
    weight = jnp.concatenate([weight] * per, axis=1)

    @pl.loop(0, ups)
    def _(i):
        up_copy(i).wait()
        x = jnp.dot(normed[...], ring[1 + i], preferred_element_type=jnp.float32)
        inner = 0.7978845608028654 * (x + 0.044715 * (x * x * x))
        hidden[:, block(i)] = ((x * (0.5 * (1.0 + jnp.tanh(inner)))) * weight).astype(jnp.bfloat16)

        @pl.when(i < downs - early - 1)
        def _():
            down_copy(early + 1 + i).start()

    def sends(pair):
        return [
            to_peer(
                d, packed.at[pair, lax.rem(me + d, n)], parts.at[pair, me],
                part_send.at[pair, d], part_recv.at[pair, d],
            )
            for d in range(1, n)
        ]

    @pl.loop(0, pairs)
    def _(pair):
        for half in range(2):
            i = pair * 2 + half
            down_copy(i).wait()
            y = jnp.dot(
                hidden[...], ring[lax.rem(1 + ups + i, RING)], preferred_element_type=jnp.float32
            )
            for step in range(STEPS):
                for q in range(per):
                    stage[:, (step * 2 + half) * per + q, :] = y[
                        step * n : (step + 1) * n, q * LANES : (q + 1) * LANES
                    ]
        packed[pair] = stage[...].astype(jnp.bfloat16)
        parts[pair, me] = packed[pair, me]
        for copy in sends(pair):
            copy.start()

    @pl.loop(0, pairs)
    def _(pair):
        for copy in sends(pair):
            copy.wait()
        halves[0, pair] = jnp.sum(parts[pair].astype(jnp.float32), axis=0)

    final = to_core(halves.at[0], halves.at[1], half_send, half_recv)
    final.start()
    final.wait()
    total_ref[...] = halves[0] + halves[1]


def fits(local_rows, mixer_width, columns, out_columns, hidden_width):
    return (
        local_rows == 1
        and lax.axis_size("expert") * STEPS == 16
        and lax.axis_size("head") == 2
        and out_columns == WIDE
        and mixer_width == columns == hidden_width == WIDE * lax.axis_size("expert")
    )


def in_kernel(mixer, stream, expert_ids, expert_gates, out_weight, norm_gain, up_weight, down_weight):
    n = lax.axis_size("expert")
    columns = stream.shape[2]
    width = up_weight.shape[1]
    downs = columns // WIDE
    per = WIDE // LANES
    table = jnp.sum(
        jnp.where(
            expert_ids[:, 0, :, None] == jnp.arange(EXPERTS)[None, None, :],
            expert_gates[:, 0, :, None].astype(jnp.float32),
            jnp.float32(0.0),
        ),
        axis=1,
    )
    target = (jnp.arange(n) * lax.axis_size("head") + lax.axis_index("head")) * width // FF
    gates = jnp.sum(
        jnp.where(target[:, None, None] == jnp.arange(EXPERTS), table[None], jnp.float32(0.0)), axis=2
    )
    lines = jnp.transpose(
        stream.astype(jnp.float32).reshape(STEPS, n, per, LANES), (1, 0, 2, 3)
    ).reshape(n, STEPS * per, LANES)
    aux = jnp.concatenate(
        [
            lines,
            jnp.broadcast_to(gates[:, :, None], (n, STEPS, LANES)),
            jnp.zeros((n, 16 - STEPS * per - STEPS, LANES), jnp.float32),
        ],
        axis=1,
    )
    token = STEPS * n
    vmem = pl.BlockSpec(memory_space=pltpu.VMEM)
    hbm = pl.BlockSpec(memory_space=pl.ANY)
    dma = pltpu.SemaphoreType.DMA
    f32, bf16 = jnp.float32, jnp.bfloat16
    total, middle = pl.pallas_call(
        functools.partial(layer_kernel, n),
        out_shape=(
            jax.ShapeDtypeStruct((downs // 2, token, LANES), f32),
            jax.ShapeDtypeStruct((STEPS, columns), f32),
        ),
        in_specs=[vmem, vmem, vmem, hbm, hbm, hbm],
        out_specs=(vmem, vmem),
        scratch_shapes=[
            pltpu.VMEM((RING, columns, WIDE), bf16),
            pltpu.VMEM((n, token, WIDE), bf16),
            pltpu.VMEM((n, 16, LANES), f32),
            pltpu.VMEM((n, token, WIDE), f32),
            pltpu.VMEM((token, columns), f32),
            pltpu.VMEM((token, WIDE), f32),
            pltpu.VMEM((token, WIDE), f32),
            pltpu.VMEM((n, token, WIDE), bf16),
            pltpu.VMEM((token, columns), bf16),
            pltpu.VMEM((token, columns), f32),
            pltpu.VMEM((token, width), bf16),
            pltpu.VMEM((n, token, LANES), f32),
            pltpu.VMEM((downs // 2, n, token, LANES), bf16),
            pltpu.VMEM((downs // 2, n, token, LANES), bf16),
            pltpu.VMEM((2, downs // 2, token, LANES), f32),
            dma((1 + width // WIDE + downs,)),
            dma((n,)), dma((n,)), dma((n,)), dma((n,)), dma, dma,
            dma((n,)), dma((n,)), dma((downs // 2, n)), dma((downs // 2, n)), dma, dma,
        ],
        compiler_params=pltpu.CompilerParams(
            collective_id=0, has_side_effects=True, vmem_limit_bytes=60 << 20
        ),
    )(
        mixer.reshape(token, WIDE), aux, norm_gain[None, :], out_weight, up_weight, down_weight
    )
    moe = jnp.transpose(
        total.reshape(downs // 2, STEPS, 2 * per, LANES), (1, 0, 2, 3)
    ).reshape(STEPS, 1, columns)
    return (middle[:, None, :] + moe).astype(bf16)


def on_device(
    stream,
    heads_in,
    heads_gate,
    write_key,
    read_query,
    step_size,
    state_cache,
    decay_rate,
    skip_gain,
    out_weight,
    norm_gain,
    up_weight,
    down_weight,
    expert_ids,
    expert_gates,
):
    local_rows = heads_in.shape[1]
    local_width = heads_in.shape[2]
    local_heads = decay_rate.shape[0]
    state = state_cache.astype(jnp.float32).reshape(local_rows, local_heads, P_SIZE, N)
    position = lax.axis_index("expert") * lax.axis_size("head") + lax.axis_index("head")
    owner = position * up_weight.shape[1] // FF
    mixers = []
    for step in range(STEPS):
        values = heads_in[step].astype(jnp.float32).reshape(local_rows, local_heads, P_SIZE)
        delta = step_size[step]
        keys = write_key[step].astype(jnp.float32)
        query = read_query[step].astype(jnp.float32)
        factor = jnp.exp(-delta * decay_rate[None, :])
        state = (
            factor[:, :, None, None] * state
            + (delta[:, :, None] * values)[:, :, :, None] * keys[:, None, None, :]
        )
        read = (
            jnp.einsum("thpn,tn->thp", state, query, precision=lax.Precision.HIGHEST)
            + skip_gain[None, :, None] * values
        )
        gate = heads_gate[step].astype(jnp.float32).reshape(local_rows, local_heads, P_SIZE)
        mixers.append((read * jax.nn.silu(gate)).reshape(local_rows, local_width).astype(jnp.bfloat16))
    if fits(local_rows, local_width, stream.shape[2], out_weight.shape[1], up_weight.shape[1]):
        return in_kernel(
            jnp.stack(mixers),
            stream,
            expert_ids,
            expert_gates,
            out_weight,
            norm_gain,
            up_weight,
            down_weight,
        )
    return finish(
        jnp.stack(mixers),
        stream,
        expert_ids,
        expert_gates,
        out_weight,
        norm_gain,
        up_weight,
        down_weight,
        owner,
    )


def solution(mesh):
    placed = (
        P(None, ("groups", "expert"), None),
        P(None, ("groups", "expert"), "head"),
        P(None, ("groups", "expert"), "head"),
        P(None, ("groups", "expert"), None),
        P(None, ("groups", "expert"), None),
        P(None, ("groups", "expert"), "head"),
        P(("groups", "expert"), "head", None),
        P("head"),
        P("head"),
        P("head", "expert"),
        P(),
        P(None, ("expert", "head")),
        P(("expert", "head"), None),
        P(None, ("groups", "expert"), None),
        P(None, ("groups", "expert"), None),
    )
    return jax.shard_map(
        on_device,
        mesh=mesh,
        in_specs=placed,
        out_specs=P(None, ("groups", "expert"), None),
        check_vma=False,
    )
```

```python
import functools
import jax
import jax.numpy as jnp
from jax import lax
from jax.experimental import pallas as pl
from jax.experimental.pallas import tpu as pltpu
from jax.sharding import PartitionSpec as P

P_SIZE = 64
N = 64
EXPERTS = 4
FF = 16384
STEPS = 2


EPSILON = 1e-05


def finish(
    mixer, stream, expert_ids, expert_gates, out_weight, norm_gain, up_weight, down_weight, owner
):
    partial_out = jnp.einsum(
        "srk,kc->src",
        lax.all_gather(mixer, "expert", axis=1, tiled=True),
        out_weight,
        preferred_element_type=jnp.float32,
    )
    summed = lax.psum(partial_out, "head")
    mixed = lax.all_to_all(summed, "expert", split_axis=1, concat_axis=2, tiled=True)
    middle = (stream.astype(jnp.float32) + mixed).astype(jnp.bfloat16)
    wide = middle.astype(jnp.float32)
    scale = lax.rsqrt(jnp.mean(wide * wide, axis=-1, keepdims=True) + EPSILON)
    normed = (wide * scale * norm_gain[None, None, :]).astype(jnp.bfloat16)
    experts = lax.broadcasted_iota(jnp.int32, (1, 1, 1, EXPERTS), 3)
    table = jnp.sum(
        jnp.where(
            expert_ids[:, :, :, None] == experts,
            expert_gates[:, :, :, None].astype(jnp.float32),
            jnp.float32(0.0),
        ),
        axis=2,
    ).astype(jnp.bfloat16)
    every_token, every_table = (
        lax.all_gather(normed, "expert", axis=1, tiled=True),
        lax.all_gather(table, "expert", axis=1, tiled=True),
    )
    picker = lax.broadcasted_iota(jnp.int32, (1, 1, EXPERTS), 2) == owner
    weight_row = jnp.sum(
        jnp.where(picker, every_table.astype(jnp.float32), jnp.float32(0.0)), axis=2
    )
    lifted = jnp.einsum("std,dc->tsc", every_token, up_weight, preferred_element_type=jnp.float32)
    hidden = (jax.nn.gelu(lifted) * jnp.transpose(weight_row)[:, :, None]).astype(jnp.bfloat16)
    combined = lax.psum_scatter(
        jnp.einsum("tsc,cd->tsd", hidden, down_weight, preferred_element_type=jnp.float32),
        "expert",
        scatter_dimension=0,
        tiled=True,
    )
    total = lax.psum(combined, "head")
    return (wide + jnp.transpose(total, (1, 0, 2))).astype(jnp.bfloat16)


LANES = 128
WIDE = 512
RING = 13


def layer_kernel(
    n,
    facts_ref, values_ref, gate_ref, aux_ref, gain_ref, state_in, out_w, up_w, down_w,
    total_ref, middle_ref,
    state, queries, spread, lines, mixed, mixer_ref, ring, mixers, auxes, unpacked, rows, mine, theirs, blocks, normed, wide, hidden,
    stage, packed, parts, halves,
    state_sem, weight_sem, mix_send, mix_recv, aux_send, aux_recv, core_send, core_recv,
    mid_send, mid_recv, part_send, part_recv, half_send, half_recv,
):
    me = lax.axis_index("expert")
    other = 1 - lax.axis_index("head")
    ups = up_w.shape[1] // WIDE
    downs = down_w.shape[1] // WIDE
    pairs = downs // 2
    columns = n * WIDE

    def block(i):
        return pl.ds(pl.multiple_of(i * WIDE, WIDE), WIDE)

    def out_copy():
        return pltpu.make_async_copy(out_w, ring.at[0], weight_sem.at[0])

    def up_copy(i):
        return pltpu.make_async_copy(up_w.at[:, block(i)], ring.at[1 + i], weight_sem.at[1 + i])

    def down_copy(i):
        at = 1 + ups + i
        return pltpu.make_async_copy(
            down_w.at[:, block(i)], ring.at[lax.rem(at, RING)], weight_sem.at[at]
        )

    state_copy = pltpu.make_async_copy(state_in, state, state_sem)
    state_copy.start()
    early = RING - 1 - ups
    out_copy().start()
    pl.loop(0, ups)(lambda i: up_copy(i).start())
    pl.loop(0, early)(lambda i: down_copy(i).start())

    barrier = pltpu.get_barrier_semaphore()
    for d in range(1, n):
        pl.semaphore_signal(
            barrier, inc=1, device_id={"expert": lax.rem(me + d, n)},
            device_id_type=pl.DeviceIdType.MESH,
        )
    pl.semaphore_signal(
        barrier, inc=1, device_id={"head": other}, device_id_type=pl.DeviceIdType.MESH
    )

    heads, half = facts_ref.shape[1], P_SIZE
    eye = lax.broadcasted_iota(jnp.int32, (heads, heads), 0) == lax.broadcasted_iota(
        jnp.int32, (heads, heads), 1
    )

    def column(row):
        return jnp.sum(jnp.where(eye, facts_ref[row : row + 1, :], 0.0), axis=1, keepdims=True)

    def meet(key, query):
        return jnp.sum(
            facts_ref[4 + key : 5 + key, :] * facts_ref[6 + query : 7 + query, :],
            axis=1, keepdims=True,
        )

    lane = lax.broadcasted_iota(jnp.int32, (heads, 2 * half), 1)
    before = lane < half

    def both(a, b):
        return jnp.where(before, a, b)

    query = both(column(6), column(7))
    place = lax.rem(lane, half)
    for p in range(P_SIZE):
        queries[p * N : (p + 1) * N, :] = jnp.where(place == p, query, 0.0).astype(jnp.bfloat16)
    delta0, delta1, decay, skip = column(0), column(1), column(2), column(3)
    factor0, factor1 = jnp.exp(-delta0 * decay), jnp.exp(-delta1 * decay)
    spread[heads : 2 * heads, :] = both(delta0 * meet(0, 0) + skip, delta1 * meet(1, 1) + skip)
    spread[2 * heads : 3 * heads, :] = both(skip * 0.0, factor1 * delta0 * meet(0, 1))
    for at, source in enumerate((values_ref, gate_ref)):
        for step in range(STEPS):
            for k in range(n):
                lines[at, step * n + k : step * n + k + 1, :] = source[
                    step : step + 1, k * WIDE : (k + 1) * WIDE
                ].astype(jnp.float32)
    state_copy.wait()
    spread[0:heads, :] = jnp.dot(
        state[...], queries[...], preferred_element_type=jnp.float32
    ) * both(factor0, factor0 * factor1)
    for j in range(WIDE // LANES):

        def pick(kind):
            even = spread[pl.ds(kind * heads + 2 * j, n, stride=WIDE // P_SIZE), :]
            odd = spread[pl.ds(kind * heads + 2 * j + 1, n, stride=WIDE // P_SIZE), :]
            return (
                jnp.concatenate([even[:, :half], odd[:, :half]], axis=1),
                jnp.concatenate([even[:, half:], odd[:, half:]], axis=1),
            )

        at = slice(j * LANES, (j + 1) * LANES)
        read, own, past = pick(0), pick(1), pick(2)
        value0, value1 = lines[0, 0:n, at], lines[0, n : 2 * n, at]
        gate0, gate1 = lines[1, 0:n, at], lines[1, n : 2 * n, at]
        mixed[0:n, at] = (read[0] + own[0] * value0) * (gate0 / (1.0 + jnp.exp(-gate0)))
        mixed[n : 2 * n, at] = (read[1] + own[1] * value1 + past[1] * value0) * (
            gate1 / (1.0 + jnp.exp(-gate1))
        )
    mixer_ref[...] = mixed[...].astype(jnp.bfloat16)
    pl.semaphore_wait(barrier, n)

    def to_peer(d, src, dst, send, recv):
        return pltpu.make_async_remote_copy(
            src_ref=src, dst_ref=dst, send_sem=send, recv_sem=recv,
            device_id={"expert": lax.rem(me + d, n)}, device_id_type=pl.DeviceIdType.MESH,
        )

    def to_core(src, dst, send, recv):
        return pltpu.make_async_remote_copy(
            src_ref=src, dst_ref=dst, send_sem=send, recv_sem=recv,
            device_id={"head": other}, device_id_type=pl.DeviceIdType.MESH,
        )

    mix = [
        to_peer(d, mixer_ref, mixers.at[me], mix_send.at[d], mix_recv.at[d]) for d in range(1, n)
    ]
    aux = [
        to_peer(d, aux_ref.at[lax.rem(me + d, n)], auxes.at[me], aux_send.at[d], aux_recv.at[d])
        for d in range(1, n)
    ]
    for copy in mix + aux:
        copy.start()
    mixers[me] = mixer_ref[...]
    auxes[me] = aux_ref[me]
    for copy in mix:
        copy.wait()
    unpacked[...] = mixers[...].astype(jnp.float32)
    for step in range(STEPS):
        for k in range(n):
            rows[step * n : (step + 1) * n, k * WIDE : (k + 1) * WIDE] = unpacked[:, step * n + k, :]

    out_copy().wait()
    mine[...] = jnp.dot(
        rows[...].astype(jnp.bfloat16), ring[0], preferred_element_type=jnp.float32
    )
    down_copy(early).start()
    swap = to_core(mine, theirs, core_send, core_recv)
    swap.start()
    for copy in aux:
        copy.wait()
    swap.wait()
    per = WIDE // LANES
    for step in range(STEPS):
        for q in range(per):
            at = slice(step * n, (step + 1) * n), slice(q * LANES, (q + 1) * LANES)
            mine[at] = auxes[:, step * per + q, :] + (mine[at] + theirs[at])
    blocks[me] = mine[...].astype(jnp.bfloat16)
    mid = [
        to_peer(d, blocks.at[me], blocks.at[me], mid_send.at[d], mid_recv.at[d])
        for d in range(1, n)
    ]
    for copy in mid:
        copy.start()
    for copy in mid:
        copy.wait()
    square = jnp.zeros((STEPS * n, WIDE), jnp.float32)
    for k in range(n):
        part = blocks[k].astype(jnp.float32)
        wide[:, k * WIDE : (k + 1) * WIDE] = part
        square += part * part
    scale = lax.rsqrt(jnp.sum(square, axis=-1, keepdims=True) / columns + EPSILON)
    for k in range(n):
        at = slice(None), slice(k * WIDE, (k + 1) * WIDE)
        normed[at] = (wide[at] * scale * gain_ref[:, k * WIDE : (k + 1) * WIDE]).astype(jnp.bfloat16)
    for step in range(STEPS):
        middle_ref[step : step + 1, :] = wide[pl.ds(step * n + me, 1), :]
    first = STEPS * per
    weight = jnp.concatenate(
        [auxes[:, first + step, :] for step in range(STEPS)], axis=0
    )
    weight = jnp.concatenate([weight] * per, axis=1)

    @pl.loop(0, ups)
    def _(i):
        up_copy(i).wait()
        x = jnp.dot(normed[...], ring[1 + i], preferred_element_type=jnp.float32)
        inner = 0.7978845608028654 * (x + 0.044715 * (x * x * x))
        hidden[:, block(i)] = ((x * (0.5 * (1.0 + jnp.tanh(inner)))) * weight).astype(jnp.bfloat16)

        @pl.when(i < downs - early - 1)
        def _():
            down_copy(early + 1 + i).start()

    def sends(pair):
        return [
            to_peer(
                d, packed.at[pair, lax.rem(me + d, n)], parts.at[pair, me],
                part_send.at[pair, d], part_recv.at[pair, d],
            )
            for d in range(1, n)
        ]

    @pl.loop(0, pairs)
    def _(pair):
        for half in range(2):
            i = pair * 2 + half
            down_copy(i).wait()
            y = jnp.dot(
                hidden[...], ring[lax.rem(1 + ups + i, RING)], preferred_element_type=jnp.float32
            )
            for step in range(STEPS):
                for q in range(per):
                    stage[:, (step * 2 + half) * per + q, :] = y[
                        step * n : (step + 1) * n, q * LANES : (q + 1) * LANES
                    ]
        packed[pair] = stage[...].astype(jnp.bfloat16)
        parts[pair, me] = packed[pair, me]
        for copy in sends(pair):
            copy.start()

    @pl.loop(0, pairs)
    def _(pair):
        for copy in sends(pair):
            copy.wait()
        halves[0, pair] = jnp.sum(parts[pair].astype(jnp.float32), axis=0)

    final = to_core(halves.at[0], halves.at[1], half_send, half_recv)
    final.start()
    final.wait()
    total_ref[...] = halves[0] + halves[1]


def fits(local_rows, mixer_width, columns, out_columns, hidden_width):
    return (
        local_rows == 1
        and lax.axis_size("expert") * STEPS == 16
        and lax.axis_size("head") == 2
        and out_columns == WIDE
        and mixer_width == columns == hidden_width == WIDE * lax.axis_size("expert")
    )


def in_kernel(
    stream,
    heads_in,
    heads_gate,
    write_key,
    read_query,
    step_size,
    state_cache,
    decay_rate,
    skip_gain,
    out_weight,
    norm_gain,
    up_weight,
    down_weight,
    expert_ids,
    expert_gates,
):
    n = lax.axis_size("expert")
    columns = stream.shape[2]
    width = up_weight.shape[1]
    downs = columns // WIDE
    per = WIDE // LANES
    table = jnp.sum(
        jnp.where(
            expert_ids[:, 0, :, None] == jnp.arange(EXPERTS)[None, None, :],
            expert_gates[:, 0, :, None].astype(jnp.float32),
            jnp.float32(0.0),
        ),
        axis=1,
    )
    target = (jnp.arange(n) * lax.axis_size("head") + lax.axis_index("head")) * width // FF
    gates = jnp.sum(
        jnp.where(target[:, None, None] == jnp.arange(EXPERTS), table[None], jnp.float32(0.0)), axis=2
    )
    lines = jnp.transpose(
        stream.astype(jnp.float32).reshape(STEPS, n, per, LANES), (1, 0, 2, 3)
    ).reshape(n, STEPS * per, LANES)
    aux = jnp.concatenate(
        [
            lines,
            jnp.broadcast_to(gates[:, :, None], (n, STEPS, LANES)),
            jnp.zeros((n, 16 - STEPS * per - STEPS, LANES), jnp.float32),
        ],
        axis=1,
    )
    token = STEPS * n
    heads = decay_rate.shape[0]
    facts = jnp.concatenate(
        [
            step_size[:, 0],
            decay_rate[None],
            skip_gain[None],
            write_key[:, 0].astype(jnp.float32),
            read_query[:, 0].astype(jnp.float32),
        ],
        axis=0,
    )
    vmem = pl.BlockSpec(memory_space=pltpu.VMEM)
    hbm = pl.BlockSpec(memory_space=pl.ANY)
    dma = pltpu.SemaphoreType.DMA
    f32, bf16 = jnp.float32, jnp.bfloat16
    total, middle = pl.pallas_call(
        functools.partial(layer_kernel, n),
        out_shape=(
            jax.ShapeDtypeStruct((downs // 2, token, LANES), f32),
            jax.ShapeDtypeStruct((STEPS, columns), f32),
        ),
        in_specs=[vmem, vmem, vmem, vmem, vmem, hbm, hbm, hbm, hbm],
        out_specs=(vmem, vmem),
        scratch_shapes=[
            pltpu.VMEM((heads, P_SIZE * N), bf16),
            pltpu.VMEM((P_SIZE * N, STEPS * P_SIZE), bf16),
            pltpu.VMEM((3 * heads, STEPS * P_SIZE), f32),
            pltpu.VMEM((2, token, WIDE), f32),
            pltpu.VMEM((token, WIDE), f32),
            pltpu.VMEM((token, WIDE), bf16),
            pltpu.VMEM((RING, columns, WIDE), bf16),
            pltpu.VMEM((n, token, WIDE), bf16),
            pltpu.VMEM((n, 16, LANES), f32),
            pltpu.VMEM((n, token, WIDE), f32),
            pltpu.VMEM((token, columns), f32),
            pltpu.VMEM((token, WIDE), f32),
            pltpu.VMEM((token, WIDE), f32),
            pltpu.VMEM((n, token, WIDE), bf16),
            pltpu.VMEM((token, columns), bf16),
            pltpu.VMEM((token, columns), f32),
            pltpu.VMEM((token, width), bf16),
            pltpu.VMEM((n, token, LANES), f32),
            pltpu.VMEM((downs // 2, n, token, LANES), bf16),
            pltpu.VMEM((downs // 2, n, token, LANES), bf16),
            pltpu.VMEM((2, downs // 2, token, LANES), f32),
            dma,
            dma((1 + width // WIDE + downs,)),
            dma((n,)), dma((n,)), dma((n,)), dma((n,)), dma, dma,
            dma((n,)), dma((n,)), dma((downs // 2, n)), dma((downs // 2, n)), dma, dma,
        ],
        compiler_params=pltpu.CompilerParams(
            collective_id=0, has_side_effects=True, vmem_limit_bytes=60 << 20
        ),
    )(
        facts, heads_in[:, 0], heads_gate[:, 0], aux, norm_gain[None, :], state_cache[0],
        out_weight, up_weight, down_weight,
    )
    moe = jnp.transpose(
        total.reshape(downs // 2, STEPS, 2 * per, LANES), (1, 0, 2, 3)
    ).reshape(STEPS, 1, columns)
    return (middle[:, None, :] + moe).astype(bf16)


def on_device(
    stream,
    heads_in,
    heads_gate,
    write_key,
    read_query,
    step_size,
    state_cache,
    decay_rate,
    skip_gain,
    out_weight,
    norm_gain,
    up_weight,
    down_weight,
    expert_ids,
    expert_gates,
):
    local_rows = heads_in.shape[1]
    local_width = heads_in.shape[2]
    local_heads = decay_rate.shape[0]
    if fits(local_rows, local_width, stream.shape[2], out_weight.shape[1], up_weight.shape[1]):
        return in_kernel(
            stream,
            heads_in,
            heads_gate,
            write_key,
            read_query,
            step_size,
            state_cache,
            decay_rate,
            skip_gain,
            out_weight,
            norm_gain,
            up_weight,
            down_weight,
            expert_ids,
            expert_gates,
        )
    state = state_cache.astype(jnp.float32).reshape(local_rows, local_heads, P_SIZE, N)
    position = lax.axis_index("expert") * lax.axis_size("head") + lax.axis_index("head")
    owner = position * up_weight.shape[1] // FF
    mixers = []
    for step in range(STEPS):
        values = heads_in[step].astype(jnp.float32).reshape(local_rows, local_heads, P_SIZE)
        delta = step_size[step]
        keys = write_key[step].astype(jnp.float32)
        query = read_query[step].astype(jnp.float32)
        factor = jnp.exp(-delta * decay_rate[None, :])
        state = (
            factor[:, :, None, None] * state
            + (delta[:, :, None] * values)[:, :, :, None] * keys[:, None, None, :]
        )
        read = (
            jnp.einsum("thpn,tn->thp", state, query, precision=lax.Precision.HIGHEST)
            + skip_gain[None, :, None] * values
        )
        gate = heads_gate[step].astype(jnp.float32).reshape(local_rows, local_heads, P_SIZE)
        mixers.append((read * jax.nn.silu(gate)).reshape(local_rows, local_width).astype(jnp.bfloat16))
    return finish(
        jnp.stack(mixers),
        stream,
        expert_ids,
        expert_gates,
        out_weight,
        norm_gain,
        up_weight,
        down_weight,
        owner,
    )


def solution(mesh):
    placed = (
        P(None, ("groups", "expert"), None),
        P(None, ("groups", "expert"), "head"),
        P(None, ("groups", "expert"), "head"),
        P(None, ("groups", "expert"), None),
        P(None, ("groups", "expert"), None),
        P(None, ("groups", "expert"), "head"),
        P(("groups", "expert"), "head", None),
        P("head"),
        P("head"),
        P("head", "expert"),
        P(),
        P(None, ("expert", "head")),
        P(("expert", "head"), None),
        P(None, ("groups", "expert"), None),
        P(None, ("groups", "expert"), None),
    )
    return jax.shard_map(
        on_device,
        mesh=mesh,
        in_specs=placed,
        out_specs=P(None, ("groups", "expert"), None),
        check_vma=False,
    )
```

```python
import functools
import jax
import jax.numpy as jnp
from jax import lax
from jax.experimental import pallas as pl
from jax.experimental.pallas import tpu as pltpu
from jax.sharding import PartitionSpec as P

P_SIZE = 64
N = 64
EXPERTS = 4
FF = 16384
STEPS = 2


EPSILON = 1e-05


def finish(
    mixer, stream, expert_ids, expert_gates, out_weight, norm_gain, up_weight, down_weight, owner
):
    partial_out = jnp.einsum(
        "srk,kc->src",
        lax.all_gather(mixer, "expert", axis=1, tiled=True),
        out_weight,
        preferred_element_type=jnp.float32,
    )
    summed = lax.psum(partial_out, "head")
    mixed = lax.all_to_all(summed, "expert", split_axis=1, concat_axis=2, tiled=True)
    middle = (stream.astype(jnp.float32) + mixed).astype(jnp.bfloat16)
    wide = middle.astype(jnp.float32)
    scale = lax.rsqrt(jnp.mean(wide * wide, axis=-1, keepdims=True) + EPSILON)
    normed = (wide * scale * norm_gain[None, None, :]).astype(jnp.bfloat16)
    experts = lax.broadcasted_iota(jnp.int32, (1, 1, 1, EXPERTS), 3)
    table = jnp.sum(
        jnp.where(
            expert_ids[:, :, :, None] == experts,
            expert_gates[:, :, :, None].astype(jnp.float32),
            jnp.float32(0.0),
        ),
        axis=2,
    ).astype(jnp.bfloat16)
    every_token, every_table = (
        lax.all_gather(normed, "expert", axis=1, tiled=True),
        lax.all_gather(table, "expert", axis=1, tiled=True),
    )
    picker = lax.broadcasted_iota(jnp.int32, (1, 1, EXPERTS), 2) == owner
    weight_row = jnp.sum(
        jnp.where(picker, every_table.astype(jnp.float32), jnp.float32(0.0)), axis=2
    )
    lifted = jnp.einsum("std,dc->tsc", every_token, up_weight, preferred_element_type=jnp.float32)
    hidden = (jax.nn.gelu(lifted) * jnp.transpose(weight_row)[:, :, None]).astype(jnp.bfloat16)
    combined = lax.psum_scatter(
        jnp.einsum("tsc,cd->tsd", hidden, down_weight, preferred_element_type=jnp.float32),
        "expert",
        scatter_dimension=0,
        tiled=True,
    )
    total = lax.psum(combined, "head")
    return (wide + jnp.transpose(total, (1, 0, 2))).astype(jnp.bfloat16)


LANES = 128
WIDE = 512
RING = 13


def layer_kernel(
    n,
    delta_ref, decay_ref, skip_ref, key_ref, query_ref, stream_ref, ids_ref, gates_ref,
    values_ref, gate_ref, gain_ref, state_in, out_w, up_w, down_w,
    out_ref,
    facts_ref, aux_ref, middle_ref,
    state, queries, spread, lines, mixed, mixer_ref, ring, mixers, auxes, unpacked, rows, mine, theirs, blocks, normed, wide, hidden,
    stage, packed, parts, halves,
    state_sem, weight_sem, mix_send, mix_recv, aux_send, aux_recv, core_send, core_recv,
    mid_send, mid_recv, part_send, part_recv, half_send, half_recv,
):
    me = lax.axis_index("expert")
    other = 1 - lax.axis_index("head")
    ups = up_w.shape[1] // WIDE
    downs = down_w.shape[1] // WIDE
    pairs = downs // 2
    columns = n * WIDE

    def block(i):
        return pl.ds(pl.multiple_of(i * WIDE, WIDE), WIDE)

    def out_copy():
        return pltpu.make_async_copy(out_w, ring.at[0], weight_sem.at[0])

    def up_copy(i):
        return pltpu.make_async_copy(up_w.at[:, block(i)], ring.at[1 + i], weight_sem.at[1 + i])

    def down_copy(i):
        at = 1 + ups + i
        return pltpu.make_async_copy(
            down_w.at[:, block(i)], ring.at[lax.rem(at, RING)], weight_sem.at[at]
        )

    state_copy = pltpu.make_async_copy(state_in, state, state_sem)
    state_copy.start()
    early = RING - 1 - ups
    out_copy().start()
    pl.loop(0, ups)(lambda i: up_copy(i).start())
    pl.loop(0, early)(lambda i: down_copy(i).start())

    barrier = pltpu.get_barrier_semaphore()
    for d in range(1, n):
        pl.semaphore_signal(
            barrier, inc=1, device_id={"expert": lax.rem(me + d, n)},
            device_id_type=pl.DeviceIdType.MESH,
        )
    pl.semaphore_signal(
        barrier, inc=1, device_id={"head": other}, device_id_type=pl.DeviceIdType.MESH
    )

    heads, half = facts_ref.shape[1], P_SIZE
    facts_ref[0:2, :] = delta_ref[...]
    facts_ref[2:3, :] = decay_ref[...]
    facts_ref[3:4, :] = skip_ref[...]
    facts_ref[4:6, :] = key_ref[...].astype(jnp.float32)
    facts_ref[6:8, :] = query_ref[...].astype(jnp.float32)
    quarter = WIDE // LANES
    aux_ref[...] = jnp.zeros_like(aux_ref)
    entering = stream_ref[...].astype(jnp.float32)
    chosen = gates_ref[...].astype(jnp.float32)
    for k in range(n):
        for step in range(STEPS):
            for q in range(quarter):
                first = k * WIDE + q * LANES
                at = step * quarter + q
                aux_ref[k, at : at + 1, :] = entering[step : step + 1, first : first + LANES]
        expert = (k * 2 + lax.axis_index("head")) * up_w.shape[1] // FF
        given = jnp.sum(jnp.where(ids_ref[...] == expert, chosen, 0.0), axis=1, keepdims=True)
        aux_ref[k, STEPS * quarter : STEPS * quarter + STEPS, :] = jnp.broadcast_to(
            given.astype(jnp.bfloat16).astype(jnp.float32), (STEPS, LANES)
        )
    eye = lax.broadcasted_iota(jnp.int32, (heads, heads), 0) == lax.broadcasted_iota(
        jnp.int32, (heads, heads), 1
    )

    def column(row):
        return jnp.sum(jnp.where(eye, facts_ref[row : row + 1, :], 0.0), axis=1, keepdims=True)

    def meet(key, query):
        return jnp.sum(
            facts_ref[4 + key : 5 + key, :] * facts_ref[6 + query : 7 + query, :],
            axis=1, keepdims=True,
        )

    lane = lax.broadcasted_iota(jnp.int32, (heads, 2 * half), 1)
    before = lane < half

    def both(a, b):
        return jnp.where(before, a, b)

    query = both(column(6), column(7))
    place = lax.rem(lane, half)
    for p in range(P_SIZE):
        queries[p * N : (p + 1) * N, :] = jnp.where(place == p, query, 0.0).astype(jnp.bfloat16)
    delta0, delta1, decay, skip = column(0), column(1), column(2), column(3)
    factor0, factor1 = jnp.exp(-delta0 * decay), jnp.exp(-delta1 * decay)
    spread[heads : 2 * heads, :] = both(delta0 * meet(0, 0) + skip, delta1 * meet(1, 1) + skip)
    spread[2 * heads : 3 * heads, :] = both(skip * 0.0, factor1 * delta0 * meet(0, 1))
    for at, source in enumerate((values_ref, gate_ref)):
        for step in range(STEPS):
            for k in range(n):
                lines[at, step * n + k : step * n + k + 1, :] = source[
                    step : step + 1, k * WIDE : (k + 1) * WIDE
                ].astype(jnp.float32)
    state_copy.wait()
    spread[0:heads, :] = jnp.dot(
        state[...], queries[...], preferred_element_type=jnp.float32
    ) * both(factor0, factor0 * factor1)
    for j in range(WIDE // LANES):

        def pick(kind):
            even = spread[pl.ds(kind * heads + 2 * j, n, stride=WIDE // P_SIZE), :]
            odd = spread[pl.ds(kind * heads + 2 * j + 1, n, stride=WIDE // P_SIZE), :]
            return (
                jnp.concatenate([even[:, :half], odd[:, :half]], axis=1),
                jnp.concatenate([even[:, half:], odd[:, half:]], axis=1),
            )

        at = slice(j * LANES, (j + 1) * LANES)
        read, own, past = pick(0), pick(1), pick(2)
        value0, value1 = lines[0, 0:n, at], lines[0, n : 2 * n, at]
        gate0, gate1 = lines[1, 0:n, at], lines[1, n : 2 * n, at]
        mixed[0:n, at] = (read[0] + own[0] * value0) * (gate0 / (1.0 + jnp.exp(-gate0)))
        mixed[n : 2 * n, at] = (read[1] + own[1] * value1 + past[1] * value0) * (
            gate1 / (1.0 + jnp.exp(-gate1))
        )
    mixer_ref[...] = mixed[...].astype(jnp.bfloat16)
    pl.semaphore_wait(barrier, n)

    def to_peer(d, src, dst, send, recv):
        return pltpu.make_async_remote_copy(
            src_ref=src, dst_ref=dst, send_sem=send, recv_sem=recv,
            device_id={"expert": lax.rem(me + d, n)}, device_id_type=pl.DeviceIdType.MESH,
        )

    def to_core(src, dst, send, recv):
        return pltpu.make_async_remote_copy(
            src_ref=src, dst_ref=dst, send_sem=send, recv_sem=recv,
            device_id={"head": other}, device_id_type=pl.DeviceIdType.MESH,
        )

    mix = [
        to_peer(d, mixer_ref, mixers.at[me], mix_send.at[d], mix_recv.at[d]) for d in range(1, n)
    ]
    aux = [
        to_peer(d, aux_ref.at[lax.rem(me + d, n)], auxes.at[me], aux_send.at[d], aux_recv.at[d])
        for d in range(1, n)
    ]
    for copy in mix + aux:
        copy.start()
    mixers[me] = mixer_ref[...]
    auxes[me] = aux_ref[me]
    for copy in mix:
        copy.wait()
    unpacked[...] = mixers[...].astype(jnp.float32)
    for step in range(STEPS):
        for k in range(n):
            rows[step * n : (step + 1) * n, k * WIDE : (k + 1) * WIDE] = unpacked[:, step * n + k, :]

    out_copy().wait()
    mine[...] = jnp.dot(
        rows[...].astype(jnp.bfloat16), ring[0], preferred_element_type=jnp.float32
    )
    down_copy(early).start()
    swap = to_core(mine, theirs, core_send, core_recv)
    swap.start()
    for copy in aux:
        copy.wait()
    swap.wait()
    per = WIDE // LANES
    for step in range(STEPS):
        for q in range(per):
            at = slice(step * n, (step + 1) * n), slice(q * LANES, (q + 1) * LANES)
            mine[at] = auxes[:, step * per + q, :] + (mine[at] + theirs[at])
    blocks[me] = mine[...].astype(jnp.bfloat16)
    mid = [
        to_peer(d, blocks.at[me], blocks.at[me], mid_send.at[d], mid_recv.at[d])
        for d in range(1, n)
    ]
    for copy in mid:
        copy.start()
    for copy in mid:
        copy.wait()
    square = jnp.zeros((STEPS * n, WIDE), jnp.float32)
    for k in range(n):
        part = blocks[k].astype(jnp.float32)
        wide[:, k * WIDE : (k + 1) * WIDE] = part
        square += part * part
    scale = lax.rsqrt(jnp.sum(square, axis=-1, keepdims=True) / columns + EPSILON)
    for k in range(n):
        at = slice(None), slice(k * WIDE, (k + 1) * WIDE)
        normed[at] = (wide[at] * scale * gain_ref[:, k * WIDE : (k + 1) * WIDE]).astype(jnp.bfloat16)
    for step in range(STEPS):
        middle_ref[step : step + 1, :] = wide[pl.ds(step * n + me, 1), :]
    first = STEPS * per
    weight = jnp.concatenate(
        [auxes[:, first + step, :] for step in range(STEPS)], axis=0
    )
    weight = jnp.concatenate([weight] * per, axis=1)

    @pl.loop(0, ups)
    def _(i):
        up_copy(i).wait()
        x = jnp.dot(normed[...], ring[1 + i], preferred_element_type=jnp.float32)
        inner = 0.7978845608028654 * (x + 0.044715 * (x * x * x))
        hidden[:, block(i)] = ((x * (0.5 * (1.0 + jnp.tanh(inner)))) * weight).astype(jnp.bfloat16)

        @pl.when(i < downs - early - 1)
        def _():
            down_copy(early + 1 + i).start()

    def sends(pair):
        return [
            to_peer(
                d, packed.at[pair, lax.rem(me + d, n)], parts.at[pair, me],
                part_send.at[pair, d], part_recv.at[pair, d],
            )
            for d in range(1, n)
        ]

    @pl.loop(0, pairs)
    def _(pair):
        for half in range(2):
            i = pair * 2 + half
            down_copy(i).wait()
            y = jnp.dot(
                hidden[...], ring[lax.rem(1 + ups + i, RING)], preferred_element_type=jnp.float32
            )
            for step in range(STEPS):
                for q in range(per):
                    stage[:, (step * 2 + half) * per + q, :] = y[
                        step * n : (step + 1) * n, q * LANES : (q + 1) * LANES
                    ]
        packed[pair] = stage[...].astype(jnp.bfloat16)
        parts[pair, me] = packed[pair, me]
        for copy in sends(pair):
            copy.start()

    @pl.loop(0, pairs)
    def _(pair):
        for copy in sends(pair):
            copy.wait()
        halves[0, pair] = jnp.sum(parts[pair].astype(jnp.float32), axis=0)

    final = to_core(halves.at[0], halves.at[1], half_send, half_recv)
    final.start()
    final.wait()
    for pair in range(downs // 2):
        both_cores = halves[0, pair] + halves[1, pair]
        for step in range(STEPS):
            for q in range(2 * per):
                first = (pair * 2 * per + q) * LANES
                at = slice(step, step + 1), slice(first, first + LANES)
                line = step * 2 * per + q
                middle_ref[at] = middle_ref[at] + both_cores[line : line + 1, :]
    out_ref[...] = middle_ref[...].astype(jnp.bfloat16)


def fits(local_rows, mixer_width, columns, out_columns, hidden_width):
    return (
        local_rows == 1
        and lax.axis_size("expert") * STEPS == 16
        and lax.axis_size("head") == 2
        and out_columns == WIDE
        and mixer_width == columns == hidden_width == WIDE * lax.axis_size("expert")
    )


def in_kernel(
    stream,
    heads_in,
    heads_gate,
    write_key,
    read_query,
    step_size,
    state_cache,
    decay_rate,
    skip_gain,
    out_weight,
    norm_gain,
    up_weight,
    down_weight,
    expert_ids,
    expert_gates,
):
    n = lax.axis_size("expert")
    columns = stream.shape[2]
    width = up_weight.shape[1]
    downs = columns // WIDE
    token = STEPS * n
    heads = decay_rate.shape[0]
    vmem = pl.BlockSpec(memory_space=pltpu.VMEM)
    hbm = pl.BlockSpec(memory_space=pl.ANY)
    dma = pltpu.SemaphoreType.DMA
    f32, bf16 = jnp.float32, jnp.bfloat16
    result = pl.pallas_call(
        functools.partial(layer_kernel, n),
        out_shape=jax.ShapeDtypeStruct((STEPS, columns), bf16),
        in_specs=[vmem] * 11 + [hbm] * 4,
        out_specs=vmem,
        scratch_shapes=[
            pltpu.VMEM((8, heads), f32),
            pltpu.VMEM((n, 16, LANES), f32),
            pltpu.VMEM((STEPS, columns), f32),
            pltpu.VMEM((heads, P_SIZE * N), bf16),
            pltpu.VMEM((P_SIZE * N, STEPS * P_SIZE), bf16),
            pltpu.VMEM((3 * heads, STEPS * P_SIZE), f32),
            pltpu.VMEM((2, token, WIDE), f32),
            pltpu.VMEM((token, WIDE), f32),
            pltpu.VMEM((token, WIDE), bf16),
            pltpu.VMEM((RING, columns, WIDE), bf16),
            pltpu.VMEM((n, token, WIDE), bf16),
            pltpu.VMEM((n, 16, LANES), f32),
            pltpu.VMEM((n, token, WIDE), f32),
            pltpu.VMEM((token, columns), f32),
            pltpu.VMEM((token, WIDE), f32),
            pltpu.VMEM((token, WIDE), f32),
            pltpu.VMEM((n, token, WIDE), bf16),
            pltpu.VMEM((token, columns), bf16),
            pltpu.VMEM((token, columns), f32),
            pltpu.VMEM((token, width), bf16),
            pltpu.VMEM((n, token, LANES), f32),
            pltpu.VMEM((downs // 2, n, token, LANES), bf16),
            pltpu.VMEM((downs // 2, n, token, LANES), bf16),
            pltpu.VMEM((2, downs // 2, token, LANES), f32),
            dma,
            dma((1 + width // WIDE + downs,)),
            dma((n,)), dma((n,)), dma((n,)), dma((n,)), dma, dma,
            dma((n,)), dma((n,)), dma((downs // 2, n)), dma((downs // 2, n)), dma, dma,
        ],
        compiler_params=pltpu.CompilerParams(
            collective_id=0, has_side_effects=True, vmem_limit_bytes=60 << 20
        ),
    )(
        step_size[:, 0], decay_rate[None], skip_gain[None], write_key[:, 0], read_query[:, 0],
        stream[:, 0], expert_ids[:, 0], expert_gates[:, 0], heads_in[:, 0], heads_gate[:, 0], norm_gain[None, :], state_cache[0],
        out_weight, up_weight, down_weight,
    )
    return result[:, None, :]


def on_device(
    stream,
    heads_in,
    heads_gate,
    write_key,
    read_query,
    step_size,
    state_cache,
    decay_rate,
    skip_gain,
    out_weight,
    norm_gain,
    up_weight,
    down_weight,
    expert_ids,
    expert_gates,
):
    local_rows = heads_in.shape[1]
    local_width = heads_in.shape[2]
    local_heads = decay_rate.shape[0]
    if fits(local_rows, local_width, stream.shape[2], out_weight.shape[1], up_weight.shape[1]):
        return in_kernel(
            stream,
            heads_in,
            heads_gate,
            write_key,
            read_query,
            step_size,
            state_cache,
            decay_rate,
            skip_gain,
            out_weight,
            norm_gain,
            up_weight,
            down_weight,
            expert_ids,
            expert_gates,
        )
    state = state_cache.astype(jnp.float32).reshape(local_rows, local_heads, P_SIZE, N)
    position = lax.axis_index("expert") * lax.axis_size("head") + lax.axis_index("head")
    owner = position * up_weight.shape[1] // FF
    mixers = []
    for step in range(STEPS):
        values = heads_in[step].astype(jnp.float32).reshape(local_rows, local_heads, P_SIZE)
        delta = step_size[step]
        keys = write_key[step].astype(jnp.float32)
        query = read_query[step].astype(jnp.float32)
        factor = jnp.exp(-delta * decay_rate[None, :])
        state = (
            factor[:, :, None, None] * state
            + (delta[:, :, None] * values)[:, :, :, None] * keys[:, None, None, :]
        )
        read = (
            jnp.einsum("thpn,tn->thp", state, query, precision=lax.Precision.HIGHEST)
            + skip_gain[None, :, None] * values
        )
        gate = heads_gate[step].astype(jnp.float32).reshape(local_rows, local_heads, P_SIZE)
        mixers.append((read * jax.nn.silu(gate)).reshape(local_rows, local_width).astype(jnp.bfloat16))
    return finish(
        jnp.stack(mixers),
        stream,
        expert_ids,
        expert_gates,
        out_weight,
        norm_gain,
        up_weight,
        down_weight,
        owner,
    )


def solution(mesh):
    placed = (
        P(None, ("groups", "expert"), None),
        P(None, ("groups", "expert"), "head"),
        P(None, ("groups", "expert"), "head"),
        P(None, ("groups", "expert"), None),
        P(None, ("groups", "expert"), None),
        P(None, ("groups", "expert"), "head"),
        P(("groups", "expert"), "head", None),
        P("head"),
        P("head"),
        P("head", "expert"),
        P(),
        P(None, ("expert", "head")),
        P(("expert", "head"), None),
        P(None, ("groups", "expert"), None),
        P(None, ("groups", "expert"), None),
    )
    return jax.shard_map(
        on_device,
        mesh=mesh,
        in_specs=placed,
        out_specs=P(None, ("groups", "expert"), None),
        check_vma=False,
    )
```
